32 devices in a mesh: dp: 8 (over z, y), head: 4 (over x, core).
Axes of the slice: x: 2, y: 2, z: 4, core: 2. Of those that a mesh axis runs over, the one named last changes fastest.
Arguments:
- hidden_in: bfloat16 [2048, 2048], P(('dp', 'head')), may hold values from -6 to 6
- norm_gain: bfloat16 [2048], replicated, may hold values from 0.25 to 1.75
- w_query: bfloat16 [2048, 2048], P(None, 'head'), may hold values from -0.125 to 0.125
- key_weight: bfloat16 [2048, 1024], P(None, 'head'), may hold values from -0.125 to 0.125
- w_value: bfloat16 [2048, 1024], P(None, 'head'), may hold values from -0.125 to 0.125
- query_gain: bfloat16 [128], replicated, may hold values from 0.796875 to 4
- key_gain: bfloat16 [128], replicated, may hold values from 0.25 to 1.75
- w_out: bfloat16 [2048, 2048], P('head'), may hold values from -0.125 to 0.125
- prefix_root_keys: bfloat16 [1024, 1024], P('dp', 'head'), may hold values from -210 to 210
- prefix_root_values: bfloat16 [1024, 1024], P('dp', 'head'), may hold values from -6 to 6
- mid_keys: bfloat16 [4096, 1024], P('dp', 'head'), may hold values from -210 to 210
- mid_values: bfloat16 [4096, 1024], P('dp', 'head'), may hold values from -6 to 6
- mid_lengths: int32 [16], replicated, may hold values from 1 to 256, 2048 in all
- leaf_keys: bfloat16 [4096, 1024], P('dp', 'head'), may hold values from -6 to 6
- leaf_values: bfloat16 [4096, 1024], P('dp', 'head'), may hold values from -6 to 6
- leaf_lengths: int32 [64], P('dp'), may hold values from 1 to 64, 2048 in all
- token_request: int32 [8, 256], P('dp'), may hold values from 0 to 7, never falling along the last dimension, each value on 1 to 64 neighbouring positions
- request_node: int32 [8, 8], P('dp'), may hold values from 0 to 15, as said below
Outputs:
- attn_update: bfloat16 [2048, 2048], P(('dp', 'head'))
- cache_keys: bfloat16 [2048, 1024], P('dp', 'head')
- cache_values: bfloat16 [2048, 1024], P('dp', 'head')
The draws below stay inside these ranges and needn't reach their ends.
Inputs may be any that keep to these rules, and one draw needn't show every extreme that they name: `token_request`: in each row requests 0 to 7 all occur, in rising order, each on 1 to 64 consecutive tokens; some request has exactly 64. `request_node`: node v is held by dp index v // 2; the 8 requests of one row have parents on 8 different dp indices, one each.
All inputs are finite; a program needn't handle non-finite values. No bound on the sum of `leaf_lengths` on one device may be relied on, other than what follows from the above.
Results may differ from the reference program's by a relative error of at most 0.039.
Values may be sent and summed in bfloat16 or wider, within the bound.
A program may use at most 128 MiB of HBM per device.

```python
import math
import jax
import jax.numpy as jnp
import numpy as np
from jax import lax

D = 2048
QUERY_HEAD_COUNT = 16
KEY_VALUE_HEADS = 8
HEAD_SIZE = 128
MID_DEV = 2
MID_LEN = 256
MAX_LEAF_KEYS = 64
SHARD_TOKENS = 256
TOKENS = 2048
REQUEST_COUNT = 8
REQS = 64
MAX_NEW_TOKENS = 64
ROOT_KEY_COUNT = 1024
MIDS = 16
QUERY_FEATURES = 2048
KVW = 1024
N_DP = 8
N_HEAD = 4


def draw_prefix_root_keys(key, part):
    return jax.random.normal(key, (ROOT_KEY_COUNT, KVW), jnp.float32).astype(jnp.bfloat16)


def draw_mid_keys(key, part):
    return jax.random.normal(key, (MIDS * MID_LEN, KVW), jnp.float32).astype(jnp.bfloat16)


def draw_request_node(key, part):
    owner_key, slot_key = jax.random.split(jax.random.fold_in(key, 17))
    row_keys = jax.random.split(owner_key, N_DP)
    owners = jax.vmap(lambda row_key: jax.random.permutation(row_key, N_DP))(row_keys)
    slots = jax.random.randint(slot_key, (N_DP, REQUEST_COUNT), 0, MID_DEV)
    return (owners * MID_DEV + slots).astype(jnp.int32)


def levels(stream_key, dims, cuts, smallest, high):
    level, own = 1.0, jax.random.fold_in(stream_key, 6)
    for dim, shards_of in cuts:
        heights = jnp.exp(jax.random.uniform(jax.random.fold_in(own, dim), (shards_of,), jnp.float32, smallest / len(cuts), high / len(cuts)))
        level = level * jnp.repeat(heights, dims[dim] // shards_of).reshape([-1 if axis == dim else 1 for axis in range(len(dims))])
    return level


def split_up(number_of, total, bound, lean):
    loads = [(1 << 20) // math.isqrt(rank ** lean) + 1 for rank in range(2, number_of + 1)]
    spare, given = total - bound - (number_of - 1), [1] * (number_of - 1)
    while spare > 0:
        free = [i for i in range(number_of - 1) if given[i] < bound]
        pool, remaining = sum([loads[i] for i in free]), spare
        for i in free:
            addition = min(bound - given[i], max(1, remaining * loads[i] // pool), spare)
            given[i] = given[i] + addition
            spare = spare - addition
    return np.array([bound] + given)


def uneven(rng, number_of, total, reach, slope):
    if number_of == 2:
        one = jax.random.randint(rng, (), max(1, total - reach), min(reach, total - 1) + 1)
        return jnp.stack([one, total - one])
    tallies = jnp.asarray(split_up(number_of, total, reach, slope), jnp.int32)
    couples = (number_of - 1) // 2
    source_of, sink = tallies[1:1 + 2 * couples:2], tallies[2:2 + 2 * couples:2]
    margin = jnp.minimum(source_of - 1, reach - sink)
    moved = jax.random.randint(jax.random.fold_in(rng, 1), (couples,), 0, 1 << 20) % (margin + 1)
    tallies = tallies.at[1:1 + 2 * couples:2].set(source_of - moved).at[2:2 + 2 * couples:2].set(sink + moved)
    return tallies[jax.random.permutation(jax.random.fold_in(rng, 2), number_of)]


def scatter_about(stream_key, extent, deviation, bound, cuts=(), dtype=jnp.bfloat16):
    result = deviation * jax.random.normal(stream_key, extent, jnp.float32)
    if cuts:
        result = result * levels(stream_key, extent, cuts, -0.22, 0.18)
    return jnp.clip(result, -bound, bound).astype(dtype)


def setup_inputs(seed: int = 0) -> dict:
    seeds = jax.random.split(jax.random.key(seed), 19)
    hidden_in = scatter_about(seeds[0], (TOKENS, D), 1.0, 6.0, ((0, 32),))
    norm_gain = jnp.clip(1.0 + 0.15 * jax.random.normal(seeds[1], (D,), jnp.float32), 0.25, 1.75).astype(jnp.bfloat16)
    w_query = scatter_about(seeds[2], (D, QUERY_FEATURES), D ** -0.5, 0.125, ((1, 4),))
    key_weight = scatter_about(seeds[3], (D, KVW), D ** -0.5, 0.125, ((1, 4),))
    w_value = scatter_about(seeds[4], (D, KVW), D ** -0.5, 0.125, ((1, 4),))
    query_gain = jnp.clip(jnp.exp(jax.random.uniform(seeds[5], (HEAD_SIZE,), jnp.float32, math.log(0.796875), math.log(4.0))), 0.796875, 4.0).astype(jnp.bfloat16)
    key_gain = jnp.clip(1.0 + 0.15 * jax.random.normal(seeds[6], (HEAD_SIZE,), jnp.float32), 0.25, 1.75).astype(jnp.bfloat16)
    w_out = scatter_about(seeds[7], (QUERY_FEATURES, D), QUERY_FEATURES ** -0.5, 0.125, ((0, 4),))
    prefix_root_keys = draw_prefix_root_keys(jax.random.fold_in(seeds[18], 71), 0)
    prefix_root_values = scatter_about(seeds[9], (ROOT_KEY_COUNT, KVW), 1.0, 6.0, ((0, 8), (1, 4)))
    mid_keys = draw_mid_keys(jax.random.fold_in(seeds[18], 71), 0)
    mid_values = scatter_about(seeds[11], (MIDS * MID_LEN, KVW), 1.0, 6.0, ((0, 8), (1, 4)))
    mid_lengths = uneven(seeds[12], MIDS, MIDS * MID_LEN // 2, MID_LEN, 2).astype(jnp.int32)
    leaf_keys = scatter_about(seeds[13], (REQS * MAX_LEAF_KEYS, KVW), 1.0, 6.0, ((0, 8), (1, 4)))
    leaf_values = scatter_about(seeds[14], (REQS * MAX_LEAF_KEYS, KVW), 1.0, 6.0, ((0, 8), (1, 4)))
    leaf_lengths = uneven(seeds[15], REQS, REQS * MAX_LEAF_KEYS // 2, MAX_LEAF_KEYS, 2).astype(jnp.int32)
    token_request = jax.vmap(lambda own: jnp.searchsorted(jnp.cumsum(uneven(own, REQUEST_COUNT, SHARD_TOKENS, MAX_NEW_TOKENS, 2)), jnp.arange(SHARD_TOKENS), side="right"))(jax.random.split(seeds[16], N_DP)).reshape((N_DP, SHARD_TOKENS)).astype(jnp.int32)
    request_node = draw_request_node(jax.random.fold_in(seeds[18], 71), 0)
    return {"hidden_in": hidden_in, "norm_gain": norm_gain, "w_query": w_query, "key_weight": key_weight, "w_value": w_value, "query_gain": query_gain, "key_gain": key_gain, "w_out": w_out, "prefix_root_keys": prefix_root_keys, "prefix_root_values": prefix_root_values, "mid_keys": mid_keys, "mid_values": mid_values, "mid_lengths": mid_lengths, "leaf_keys": leaf_keys, "leaf_values": leaf_values, "leaf_lengths": leaf_lengths, "token_request": token_request, "request_node": request_node}


EPS = 1e-06
THETA = 1000000.0
MASKED = -1e+30

def rms_rows(values, gain):
    power = lax.optimization_barrier(jnp.mean(values * values, axis=-1, keepdims=True))
    return values * lax.rsqrt(power + EPS) * gain

def rotate(values, positions):
    width = values.shape[-1]
    half = width // 2
    exponent = jnp.arange(half).astype(jnp.float32) * (2.0 / width)
    freqs = jnp.power(THETA, -exponent)
    angles = positions.astype(jnp.float32)[:, None] * freqs[None, :]
    cosine = jnp.cos(angles)[:, None, :]
    sine = jnp.sin(angles)[:, None, :]
    first = values[..., :half]
    second = values[..., half:]
    return jnp.concatenate([first * cosine - second * sine, second * cosine + first * sine], axis=-1)

def rounded(weights):
    return lax.optimization_barrier(weights.astype(jnp.bfloat16)).astype(jnp.float32)

def attend_over_block(query_matrix, keys, values, lengths, kv_heads, head_dim):
    blocks, slots, width = query_matrix.shape
    query_group = width // (kv_heads * head_dim)
    span = keys.shape[1]
    heads_query = query_matrix.astype(jnp.float32).reshape(blocks, slots, kv_heads, query_group, head_dim)
    key_heads = keys.astype(jnp.float32).reshape(blocks, span, kv_heads, head_dim)
    value_heads = values.astype(jnp.float32).reshape(blocks, span, kv_heads, head_dim)
    scores = jnp.einsum('bskgd,blkd->bskgl', heads_query, key_heads) / math.sqrt(head_dim)
    live = jnp.arange(span).astype(jnp.int32)[None, :] < lengths.astype(jnp.int32)[:, None]
    scores = jnp.where(live[:, None, None, None, :], scores, MASKED)
    highest = lax.optimization_barrier(jnp.max(scores, axis=-1))
    weights = jnp.exp(scores - highest[..., None])
    total = lax.optimization_barrier(jnp.sum(weights, axis=-1))
    summed = jnp.einsum('bskgl,blkd->bskgd', rounded(weights), value_heads)
    output = (summed / total[..., None]).astype(jnp.bfloat16).reshape(blocks, slots, width)
    log_total = (highest + jnp.log(total)).reshape(blocks, slots, kv_heads * query_group)
    return (output, log_total)

def reference(hidden_in, norm_gain, w_query, key_weight, w_value, query_gain, key_gain, w_out, prefix_root_keys, prefix_root_values, mid_keys, mid_values, mid_lengths, leaf_keys, leaf_values, leaf_lengths, token_request, request_node):
    query_group = QUERY_HEAD_COUNT // KEY_VALUE_HEADS
    scale = 1.0 / math.sqrt(HEAD_SIZE)
    branch_keys = mid_keys.reshape(MIDS, MID_LEN, KVW)
    branch_values = mid_values.reshape(MIDS, MID_LEN, KVW)
    root_heads_key = prefix_root_keys.astype(jnp.float32).reshape(ROOT_KEY_COUNT, KEY_VALUE_HEADS, HEAD_SIZE)
    root_heads_value = prefix_root_values.astype(jnp.float32).reshape(ROOT_KEY_COUNT, KEY_VALUE_HEADS, HEAD_SIZE)
    request_ids = jnp.arange(REQUEST_COUNT).astype(jnp.int32)
    token_ids = jnp.arange(SHARD_TOKENS).astype(jnp.int32)
    node_ids = jnp.arange(MIDS).astype(jnp.int32)
    slot_ids = jnp.arange(MAX_NEW_TOKENS).astype(jnp.int32)
    leaf_ids = jnp.arange(REQUEST_COUNT * MAX_LEAF_KEYS).astype(jnp.int32)
    leaf_owner = leaf_ids // MAX_LEAF_KEYS
    leaf_place = leaf_ids % MAX_LEAF_KEYS
    out_blocks = w_out.astype(jnp.float32).reshape(N_HEAD, QUERY_FEATURES // N_HEAD, D)

    def one_batch(items):
        rows_in, leaf_key_rows, leaf_value_rows, leaf_len, segment, branch_nodes = items
        normalized_input = rms_rows(rows_in.astype(jnp.float32), norm_gain.astype(jnp.float32)).astype(jnp.bfloat16)
        query_part = jnp.dot(normalized_input, w_query, preferred_element_type=jnp.float32).reshape(SHARD_TOKENS, QUERY_HEAD_COUNT, HEAD_SIZE)
        key_portion = jnp.dot(normalized_input, key_weight, preferred_element_type=jnp.float32).reshape(SHARD_TOKENS, KEY_VALUE_HEADS, HEAD_SIZE)
        value_portion = jnp.dot(normalized_input, w_value, preferred_element_type=jnp.float32).astype(jnp.bfloat16)
        member = segment[None, :] == request_ids[:, None]
        counts = lax.optimization_barrier(jnp.sum(member.astype(jnp.int32), axis=1)).astype(jnp.int32)
        starts = (jnp.cumsum(counts) - counts).astype(jnp.int32)
        offset = token_ids - lax.optimization_barrier(jnp.sum(jnp.where(member, starts[:, None], 0), axis=0)).astype(jnp.int32)
        branch_length = lax.optimization_barrier(jnp.sum(jnp.where(branch_nodes[:, None] == node_ids[None, :], mid_lengths[None, :], 0), axis=1)).astype(jnp.int32)
        positions = ROOT_KEY_COUNT + lax.optimization_barrier(jnp.sum(jnp.where(member, (branch_length + leaf_len)[:, None], 0), axis=0)).astype(jnp.int32) + offset
        query_matrix = rotate(rms_rows(query_part, query_gain.astype(jnp.float32)), positions).astype(jnp.bfloat16)
        new_keys = rotate(rms_rows(key_portion, key_gain.astype(jnp.float32)), positions).astype(jnp.bfloat16)
        heads_query = query_matrix.astype(jnp.float32).reshape(SHARD_TOKENS, KEY_VALUE_HEADS, query_group, HEAD_SIZE)
        new_key_heads = new_keys.astype(jnp.float32)
        fresh_value_heads = value_portion.astype(jnp.float32).reshape(SHARD_TOKENS, KEY_VALUE_HEADS, HEAD_SIZE)
        leaf_heads_key = leaf_key_rows.astype(jnp.float32).reshape(REQUEST_COUNT * MAX_LEAF_KEYS, KEY_VALUE_HEADS, HEAD_SIZE)
        leaf_heads_value = leaf_value_rows.astype(jnp.float32).reshape(REQUEST_COUNT * MAX_LEAF_KEYS, KEY_VALUE_HEADS, HEAD_SIZE)
        root_scores = jnp.einsum('tkgd,skd->tkgs', heads_query, root_heads_key) * scale
        own_scores = jnp.einsum('tkgd,skd->tkgs', heads_query, new_key_heads) * scale
        leaf_scores = jnp.einsum('tkgd,skd->tkgs', heads_query, leaf_heads_key) * scale
        own_live = (segment[:, None] == segment[None, :]) & (token_ids[None, :] <= token_ids[:, None])
        leaf_limit = lax.optimization_barrier(jnp.sum(jnp.where(leaf_owner[None, :] == request_ids[:, None], leaf_len[:, None], 0), axis=0))
        leaf_live = (leaf_owner[None, :] == segment[:, None]) & (leaf_place < leaf_limit)[None, :]
        own_scores = jnp.where(own_live[:, None, None, :], own_scores, MASKED)
        leaf_scores = jnp.where(leaf_live[:, None, None, :], leaf_scores, MASKED)
        highest = jnp.maximum(lax.optimization_barrier(jnp.max(root_scores, axis=-1)), jnp.maximum(lax.optimization_barrier(jnp.max(own_scores, axis=-1)), lax.optimization_barrier(jnp.max(leaf_scores, axis=-1))))
        root_weights = jnp.exp(root_scores - highest[..., None])
        own_weights = jnp.where(own_live[:, None, None, :], jnp.exp(own_scores - highest[..., None]), 0.0)
        leaf_weights = jnp.where(leaf_live[:, None, None, :], jnp.exp(leaf_scores - highest[..., None]), 0.0)
        near_total = lax.optimization_barrier(jnp.sum(root_weights, axis=-1)) + lax.optimization_barrier(jnp.sum(own_weights, axis=-1)) + lax.optimization_barrier(jnp.sum(leaf_weights, axis=-1))
        near_summed = jnp.einsum('tkgs,skd->tkgd', rounded(root_weights), root_heads_value)
        near_summed = near_summed + jnp.einsum('tkgs,skd->tkgd', rounded(own_weights), fresh_value_heads)
        near_summed = near_summed + jnp.einsum('tkgs,skd->tkgd', rounded(leaf_weights), leaf_heads_value)
        valid = slot_ids[None, :] < counts[:, None]
        picks = jnp.where(valid, starts[:, None] + slot_ids[None, :], 0).astype(jnp.int32).reshape(-1)
        query_rows = query_matrix.reshape(SHARD_TOKENS, QUERY_FEATURES)
        scratch_rows = jnp.take(query_rows, picks, axis=0).reshape(REQUEST_COUNT, MAX_NEW_TOKENS, QUERY_FEATURES)
        scratch_rows = jnp.where(valid[..., None], scratch_rows, jnp.zeros((), jnp.bfloat16))
        middle_output, middle_log_sum = attend_over_block(scratch_rows, jnp.take(branch_keys, branch_nodes, axis=0), jnp.take(branch_values, branch_nodes, axis=0), branch_length, KEY_VALUE_HEADS, HEAD_SIZE)
        flattened_rows = (lax.optimization_barrier(jnp.sum(jnp.where(member, (request_ids * MAX_NEW_TOKENS)[:, None], 0), axis=0)) + offset).astype(jnp.int32)
        middle_rows = jnp.take(middle_output.reshape(REQUEST_COUNT * MAX_NEW_TOKENS, QUERY_FEATURES), flattened_rows, axis=0).astype(jnp.float32).reshape(SHARD_TOKENS, KEY_VALUE_HEADS, query_group, HEAD_SIZE)
        middle_maximum = jnp.take(middle_log_sum.reshape(REQUEST_COUNT * MAX_NEW_TOKENS, QUERY_HEAD_COUNT), flattened_rows, axis=0).reshape(SHARD_TOKENS, KEY_VALUE_HEADS, query_group)
        joint = jnp.maximum(highest, middle_maximum)
        near_part = jnp.exp(highest - joint)
        far_part = jnp.exp(middle_maximum - joint)
        attn = (near_part[..., None] * near_summed + far_part[..., None] * middle_rows) / (near_part * near_total + far_part)[..., None]
        attn = attn.reshape(SHARD_TOKENS, QUERY_FEATURES).astype(jnp.bfloat16)
        parts = jnp.einsum('tjc,jcd->jtd', attn.astype(jnp.float32).reshape(SHARD_TOKENS, N_HEAD, QUERY_FEATURES // N_HEAD), out_blocks)
        update = lax.optimization_barrier(jnp.sum(rounded(parts), axis=0)).astype(jnp.bfloat16)
        return (update, new_keys.reshape(SHARD_TOKENS, KVW), value_portion)
    updates, keys_out, values_out = lax.map(one_batch, (hidden_in.reshape(N_DP, SHARD_TOKENS, D), leaf_keys.reshape(N_DP, REQUEST_COUNT * MAX_LEAF_KEYS, KVW), leaf_values.reshape(N_DP, REQUEST_COUNT * MAX_LEAF_KEYS, KVW), leaf_lengths.reshape(N_DP, REQUEST_COUNT), token_request, request_node))
    return (updates.reshape(TOKENS, D), keys_out.reshape(TOKENS, KVW), values_out.reshape(TOKENS, KVW))
```

```python
import math

import jax
import jax.numpy as jnp
from jax import lax
from jax.sharding import PartitionSpec as P

MID_DEV = 2
MID_LEN = 256


EPS = 1e-06
THETA = 1000000.0
MASKED = -1e30


def rms_rows(values, gain):
    power = jnp.mean(values * values, axis=-1, keepdims=True)
    return values * lax.rsqrt(power + EPS) * gain


def rotate(values, positions):
    width = values.shape[-1]
    half = width // 2
    exponent = jnp.arange(half).astype(jnp.float32) * (2.0 / width)
    freqs = jnp.power(THETA, -exponent)
    angles = positions.astype(jnp.float32)[:, None] * freqs[None, :]
    cosine = jnp.cos(angles)[:, None, :]
    sine = jnp.sin(angles)[:, None, :]
    first = values[..., :half]
    second = values[..., half:]
    return jnp.concatenate(
        [first * cosine - second * sine, second * cosine + first * sine], axis=-1
    )


def body(
    hidden_in,
    norm_gain,
    w_query,
    key_weight,
    w_value,
    query_gain,
    key_gain,
    w_out,
    prefix_root_keys,
    prefix_root_values,
    mid_keys,
    mid_values,
    mid_lengths,
    leaf_keys,
    leaf_values,
    leaf_lengths,
    token_request,
    request_node,
):
    head_dim = query_gain.shape[0]
    query_width = w_query.shape[1]
    key_width = key_weight.shape[1]
    kv_heads = key_width // head_dim
    query_group = query_width // key_width
    scale = 1.0 / math.sqrt(head_dim)
    dp_count = lax.axis_size("dp")
    normalized_input = rms_rows(
        hidden_in.astype(jnp.float32), norm_gain.astype(jnp.float32)
    ).astype(jnp.bfloat16)
    piece = lax.all_gather(normalized_input, "head", axis=0, tiled=True)
    mixed = jnp.concatenate(
        [
            jnp.dot(piece, w_query, preferred_element_type=jnp.float32),
            jnp.dot(piece, key_weight, preferred_element_type=jnp.float32),
            jnp.dot(piece, w_value, preferred_element_type=jnp.float32),
        ],
        axis=1,
    )
    height = mixed.shape[0]
    segment = token_request[0]
    branch_nodes = request_node[0]
    requests = branch_nodes.shape[0]
    request_ids = jnp.arange(requests, dtype=jnp.int32)
    token_ids = jnp.arange(height, dtype=jnp.int32)
    member = segment[None, :] == request_ids[:, None]
    counts = jnp.sum(member.astype(jnp.int32), axis=1)
    earlier = request_ids[None, :] < request_ids[:, None]
    starts = jnp.sum(jnp.where(earlier, counts[None, :], 0), axis=1)
    offset = token_ids - jnp.sum(jnp.where(member, starts[:, None], 0), axis=0)
    node_total = mid_lengths.shape[0]
    node_match = branch_nodes[:, None] == jnp.arange(node_total, dtype=jnp.int32)[None, :]
    branch_length = jnp.sum(jnp.where(node_match, mid_lengths[None, :], 0), axis=1)
    root_total = prefix_root_keys.shape[0] * dp_count
    positions = (
        root_total
        + jnp.sum(jnp.where(member, (branch_length + leaf_lengths)[:, None], 0), axis=0)
        + offset
    )
    query_part = mixed[:, :query_width].reshape(height, query_width // head_dim, head_dim)
    key_portion = mixed[:, query_width : query_width + key_width].reshape(
        height, kv_heads, head_dim
    )
    query_matrix = rotate(rms_rows(query_part, query_gain.astype(jnp.float32)), positions).astype(
        jnp.bfloat16
    )
    new_keys = rotate(rms_rows(key_portion, key_gain.astype(jnp.float32)), positions).astype(
        jnp.bfloat16
    )
    new_values = mixed[:, query_width + key_width :].astype(jnp.bfloat16)
    heads_query = query_matrix.reshape(height, kv_heads, query_group, head_dim)
    root_keys = lax.all_gather(prefix_root_keys, "dp", axis=0, tiled=True)
    root_values = lax.all_gather(prefix_root_values, "dp", axis=0, tiled=True)
    owner_of = branch_nodes // MID_DEV
    owner_ids = jnp.arange(dp_count, dtype=jnp.int32)
    owner_match = owner_of[None, :] == owner_ids[:, None]
    block_slot = jnp.sum(jnp.where(owner_match, (branch_nodes % MID_DEV)[None, :], 0), axis=1)
    block_request = jnp.sum(jnp.where(owner_match, request_ids[None, :], 0), axis=1)
    block_length = jnp.sum(jnp.where(owner_match, branch_length[None, :], 0), axis=1)
    wanted = lax.all_to_all(block_slot[:, None], "dp", split_axis=0, concat_axis=0, tiled=True)[
        :, 0
    ]
    second = (wanted == 1)[:, None, None]
    own_pairs = jnp.concatenate([mid_keys, mid_values], axis=1).reshape(
        MID_DEV, MID_LEN, 2 * key_width
    )
    sent = jnp.where(second, own_pairs[1][None], own_pairs[0][None])
    got = lax.all_to_all(sent, "dp", split_axis=0, concat_axis=0, tiled=True)
    got = got.reshape(dp_count * MID_LEN, 2 * key_width)
    leaf_each = leaf_keys.shape[0] // requests
    leaf_live = jnp.arange(leaf_each, dtype=jnp.int32)[None, :] < leaf_lengths[:, None]
    leaf_tag = jnp.where(leaf_live, request_ids[:, None], -1).reshape(-1)
    mid_live = jnp.arange(MID_LEN, dtype=jnp.int32)[None, :] < block_length[:, None]
    mid_tag = jnp.where(mid_live, block_request[:, None], -1).reshape(-1)
    own_mask = (segment[None, :] == segment[:, None]) & (token_ids[None, :] <= token_ids[:, None])
    mask = jnp.concatenate(
        [
            jnp.ones((height, root_keys.shape[0]), jnp.bool_),
            leaf_tag[None, :] == segment[:, None],
            own_mask,
            mid_tag[None, :] == segment[:, None],
        ],
        axis=1,
    )
    all_keys = jnp.concatenate(
        [root_keys, leaf_keys, new_keys.reshape(height, key_width), got[:, :key_width]], axis=0
    ).reshape(-1, kv_heads, head_dim)
    all_values = jnp.concatenate(
        [root_values, leaf_values, new_values, got[:, key_width:]], axis=0
    ).reshape(-1, kv_heads, head_dim)
    scores = jnp.einsum(
        "tkgd,skd->kgts", heads_query, all_keys, preferred_element_type=jnp.float32
    )
    scores = jnp.where(mask[None, None], scores * scale, MASKED)
    weights = jnp.exp(scores - jnp.max(scores, axis=-1, keepdims=True))
    total = jnp.sum(weights, axis=-1)
    summed = jnp.einsum(
        "kgts,skd->kgtd",
        weights.astype(jnp.bfloat16),
        all_values,
        preferred_element_type=jnp.float32,
    )
    attn = (summed / total[..., None]).astype(jnp.bfloat16)
    attn = attn.transpose(2, 0, 1, 3).reshape(height, query_width)
    update = lax.psum_scatter(
        jnp.dot(attn, w_out, preferred_element_type=jnp.float32).astype(jnp.bfloat16),
        "head",
        scatter_dimension=0,
        tiled=True,
    )
    return (update, new_keys.reshape(height, key_width), new_values)


def solution(mesh):
    in_specs = (
        P(("dp", "head"), None),
        P(),
        P(None, "head"),
        P(None, "head"),
        P(None, "head"),
        P(),
        P(),
        P("head", None),
        P("dp", "head"),
        P("dp", "head"),
        P("dp", "head"),
        P("dp", "head"),
        P(),
        P("dp", "head"),
        P("dp", "head"),
        P("dp"),
        P("dp", None),
        P("dp", None),
    )
    out_specs = (P(("dp", "head"), None), P("dp", "head"), P("dp", "head"))
    return jax.shard_map(body, mesh=mesh, in_specs=in_specs, out_specs=out_specs, check_vma=False)
```

```python
import functools
import math

import jax
import jax.numpy as jnp
import numpy as np
from jax import lax
from jax.experimental import pallas as pl
from jax.experimental.pallas import tpu as pltpu
from jax.sharding import PartitionSpec as P

MID_DEV = 2
MID_LEN = 256
EPS = 1e-06
THETA = 1000000.0
MASKED = -1e30
F32 = jnp.float32
BF16 = jnp.bfloat16
MESH = pl.DeviceIdType.MESH


def kernel(
    n_dp, n_head,
    hidden, norm_gain, wq_hbm, wk_hbm, wv_hbm, query_gain, key_gain, wo_hbm, root_k, root_v,
    mid_k, mid_v, mid_len, leaf_k, leaf_v, leaf_len, seg_in, node_in, freqs,
    out, new_k, new_v,
    wq, wk, wv, wo, normed, info, roots_k, roots_v, staged, mids, queries, tags, top, acc, attn,
    parts, got, local_sem, hid_send, hid_recv, info_send, info_recv, rk_send, rk_recv, rv_send,
    rv_recv, mid_send, mid_recv, part_send, part_recv,
):
    me, mh = lax.axis_index("dp"), lax.axis_index("head")
    share = hidden.shape[0]
    height = normed.shape[0]
    requests = node_in.shape[1]
    nodes = mid_len.shape[1]
    root_rows = root_k.shape[0]
    kv_heads = wk.shape[1] // 128
    group = wq.shape[1] // wk.shape[1]
    kw = wk.shape[1]
    scale = 1.0 / math.sqrt(128)

    loads = [
        pltpu.make_async_copy(a, b, local_sem.at[i])
        for i, (a, b) in enumerate(((wq_hbm, wq), (wk_hbm, wk), (wv_hbm, wv), (wo_hbm, wo)))
    ]
    for load in loads:
        load.start()

    barrier = pltpu.get_barrier_semaphore()

    def greet_dp(d, _):
        pl.semaphore_signal(
            barrier, inc=1, device_id=(lax.rem(me + d, n_dp), mh), device_id_type=MESH
        )
        return 0

    def greet_head(d, _):
        pl.semaphore_signal(
            barrier, inc=1, device_id=(me, lax.rem(mh + d, n_head)), device_id_type=MESH
        )
        return 0

    lax.fori_loop(1, n_dp, greet_dp, 0)
    lax.fori_loop(1, n_head, greet_head, 0)

    x = hidden[...].astype(F32)
    power = jnp.mean(x * x, axis=-1, keepdims=True)
    x = (x * lax.rsqrt(power + EPS) * norm_gain[...].astype(F32)).astype(BF16)
    my_rows = pl.ds(pl.multiple_of(mh * share, share), share)
    normed[my_rows, :] = x

    eye = lax.broadcasted_iota(jnp.int32, (requests, requests), 0) == lax.broadcasted_iota(
        jnp.int32, (requests, requests), 1
    )

    def column(row):
        return jnp.sum(jnp.where(eye, row.astype(F32), 0.0), axis=1, keepdims=True)

    branch = column(node_in[...])
    info[me] = jnp.broadcast_to(branch, (requests, 128))
    my_root = pl.ds(pl.multiple_of(me * root_rows, root_rows), root_rows)
    roots_k[my_root, :] = root_k[...]
    roots_v[my_root, :] = root_v[...]

    pl.semaphore_wait(barrier, n_dp + n_head - 2)

    def hid_copy(d, source):
        rows = pl.ds(pl.multiple_of(source * share, share), share)
        return pltpu.make_async_remote_copy(
            normed.at[rows, :], normed.at[rows, :], hid_send.at[d], hid_recv.at[source],
            device_id=(me, lax.rem(mh + d, n_head)), device_id_type=MESH,
        )

    def info_copy(d, source):
        return pltpu.make_async_remote_copy(
            info.at[source], info.at[source], info_send.at[d], info_recv.at[source],
            device_id=(lax.rem(me + d, n_dp), mh), device_id_type=MESH,
        )

    def root_copies(d, source):
        rows = pl.ds(pl.multiple_of(source * root_rows, root_rows), root_rows)
        target = (lax.rem(me + d, n_dp), mh)
        return (
            pltpu.make_async_remote_copy(
                roots_k.at[rows, :], roots_k.at[rows, :], rk_send.at[d], rk_recv.at[source],
                device_id=target, device_id_type=MESH,
            ),
            pltpu.make_async_remote_copy(
                roots_v.at[rows, :], roots_v.at[rows, :], rv_send.at[d], rv_recv.at[source],
                device_id=target, device_id_type=MESH,
            ),
        )

    def mid_copy(d, source):
        return pltpu.make_async_remote_copy(
            staged.at[d], mids.at[source], mid_send.at[d], mid_recv.at[source],
            device_id=(lax.rem(me + d, n_dp), mh), device_id_type=MESH,
        )

    def part_copy(d, source):
        return pltpu.make_async_remote_copy(
            parts.at[d], got.at[source], part_send.at[d], part_recv.at[source],
            device_id=(me, lax.rem(mh + d, n_head)), device_id_type=MESH,
        )

    def over(count, act):
        def step(d, _):
            act(d)
            return 0

        lax.fori_loop(1, count, step, 0)

    over(n_dp, lambda d: info_copy(d, me).start())
    over(n_head, lambda d: hid_copy(d, mh).start())

    def send_root(d):
        for copy in root_copies(d, me):
            copy.start()

    over(n_dp, send_root)

    def chosen(who):
        wish = jnp.max(jnp.where(info[who] == (MID_DEV * me + 1).astype(F32), 1.0, 0.0), axis=0, keepdims=True)
        wish = jnp.max(wish, axis=1, keepdims=True)
        pair = [
            jnp.concatenate([mid_k[pl.ds(s * MID_LEN, MID_LEN), :], mid_v[pl.ds(s * MID_LEN, MID_LEN), :]], axis=1).astype(F32)
            for s in range(2)
        ]
        wide = jnp.broadcast_to(wish, pair[0].shape)
        return jnp.where(wide > 0.5, pair[1], pair[0]).astype(BF16)

    def send_mid(d):
        who = lax.rem(me + d, n_dp)
        info_copy(d, who).wait_recv()
        staged[d] = chosen(who)
        mid_copy(d, me).start()

    over(n_dp, send_mid)
    mids[me] = chosen(me)

    seg = seg_in[...].astype(F32)
    req = lax.broadcasted_iota(jnp.int32, (requests, height), 0).astype(F32)
    starts = jnp.sum(jnp.where(seg < req, 1.0, 0.0), axis=1, keepdims=True)
    node_ids = lax.broadcasted_iota(jnp.int32, (requests, nodes), 1).astype(F32)
    branch_len = jnp.sum(
        jnp.where(node_ids == branch, mid_len[...].astype(F32), 0.0), axis=1, keepdims=True
    )
    leaf_col = column(leaf_len[...])
    base = root_rows * n_dp + branch_len + leaf_col - starts
    pos = jnp.sum(jnp.where(seg == req, base, 0.0), axis=0, keepdims=True)
    pos = pos + lax.broadcasted_iota(jnp.int32, (1, height), 1).astype(F32)
    pos = jnp.transpose(jnp.broadcast_to(pos, (128, height)))
    seg_rep = jnp.transpose(jnp.broadcast_to(seg, (128, height)))
    lane = lax.broadcasted_iota(jnp.int32, (height, 128), 1)
    tags[...] = jnp.where(seg_rep == lane.astype(F32), 1.0, 0.0).astype(BF16)
    spread = lax.broadcasted_iota(jnp.int32, (requests, 128), 0) == lax.broadcasted_iota(
        jnp.int32, (requests, 128), 1
    )

    def lanes(col):
        return jnp.sum(jnp.where(spread, col, 0.0), axis=0, keepdims=True)

    real = jnp.sum(jnp.where(spread, 1.0, 0.0), axis=0, keepdims=True)
    leaf_row, mid_row, node_row = lanes(leaf_col), lanes(branch_len), lanes(branch)
    node_row = jnp.where(real > 0.5, node_row, -2.0)
    angle = pos * freqs[...]
    cosine = jnp.cos(angle)
    sine = jnp.sin(angle)
    sine = jnp.where(lane < 64, -sine, sine)

    over(n_head, lambda d: hid_copy(d, lax.rem(mh + d, n_head)).wait_recv())
    for load in loads:
        load.wait()
    inputs = normed[...]
    values = jnp.dot(inputs, wv[...], preferred_element_type=F32).astype(BF16)
    new_v[...] = values

    def turned(y, gain):
        power = jnp.mean(y * y, axis=-1, keepdims=True)
        y = y * lax.rsqrt(power + EPS) * gain[...].astype(F32)
        return (y * cosine + pltpu.roll(y, 64, axis=1) * sine).astype(BF16)

    for j in range(kv_heads):
        cols = slice(j * 128, j * 128 + 128)
        y = jnp.dot(inputs, wk[:, cols], preferred_element_type=F32)
        new_k[:, cols] = turned(y, key_gain)
    for j in range(kv_heads):
        for g in range(group):
            h = j * group + g
            y = jnp.dot(inputs, wq[:, h * 128 : h * 128 + 128], preferred_element_type=F32)
            queries[j, g * height : (g + 1) * height, :] = turned(y, query_gain)

    tall = group * height

    def attend(j, keys, bias, vals, first=False, causal=False):
        q = queries[j]
        if bias is not None:
            q = jnp.concatenate([q, jnp.concatenate([tags[...]] * group, axis=0)], axis=1)
            keys = jnp.concatenate([keys, bias], axis=1)
        s = lax.dot_general(q, keys, (((1,), (1,)), ((), ())), preferred_element_type=F32)
        if causal:
            row = lax.broadcasted_iota(jnp.int32, (tall, height), 0) % height
            s = jnp.where(lax.broadcasted_iota(jnp.int32, (tall, height), 1) <= row, s, MASKED)
        peak = jnp.max(s, axis=1, keepdims=True)
        if not first:
            old = top[j]
            peak = jnp.maximum(old[:, :1], peak)
        p = jnp.exp((s - peak) * scale).astype(BF16)
        wide = jnp.concatenate([vals, jnp.ones((vals.shape[0], 128), BF16)], axis=1)
        r = jnp.dot(p, wide, preferred_element_type=F32)
        full = jnp.broadcast_to(peak, (tall, 128))
        if not first:
            shrink = jnp.exp((old - full) * scale)
            r = acc[j] * jnp.concatenate([shrink, shrink], axis=1) + r
        acc[j] = r
        top[j] = full

    key_row = lax.broadcasted_iota(jnp.int32, (height, 128), 0)
    own_bias = jnp.where(tags[...].astype(F32) > 0.5, 0.0, MASKED).astype(BF16)
    for j in range(kv_heads):
        cols = slice(j * 128, j * 128 + 128)
        attend(j, new_k[:, cols], own_bias, new_v[:, cols], first=True, causal=True)
    leaf_each = leaf_k.shape[0] // requests

    def leaf_step(i, _):
        rows = pl.ds(pl.multiple_of(i * 256, 256), 256)
        at = lax.broadcasted_iota(jnp.int32, (256, 128), 0) + i * 256
        mine = lax.broadcasted_iota(jnp.int32, (256, 128), 1) == at // leaf_each
        live = (at % leaf_each).astype(F32) < leaf_row
        bias = jnp.where(mine & live, 0.0, MASKED).astype(BF16)
        for j in range(kv_heads):
            cols = slice(j * 128, j * 128 + 128)
            attend(j, leaf_k[rows, cols], bias, leaf_v[rows, cols])
        return 0

    lax.fori_loop(0, leaf_k.shape[0] // 256, leaf_step, 0)

    def mid_block(who):
        at = lax.broadcasted_iota(jnp.int32, (MID_LEN, 128), 0).astype(F32)
        first_node = (MID_DEV * who).astype(F32)
        mine = (node_row >= first_node) & (node_row < first_node + MID_DEV)
        reach = jnp.where(mine, mid_row, 0.0)
        bias = jnp.where(at < reach, 0.0, MASKED).astype(BF16)
        block = mids.at[who]
        for j in range(kv_heads):
            attend(
                j, block[:, j * 128 : j * 128 + 128], bias,
                block[:, kw + j * 128 : kw + j * 128 + 128],
            )

    mid_block(me)

    def root_wait(d):
        for copy in root_copies(d, lax.rem(me + d, n_dp)):
            copy.wait_recv()

    over(n_dp, root_wait)

    def root_step(i, _):
        rows = pl.ds(pl.multiple_of(i * 512, 512), 512)
        for j in range(kv_heads):
            cols = slice(j * 128, j * 128 + 128)
            attend(j, roots_k[rows, cols], None, roots_v[rows, cols])
        return 0

    lax.fori_loop(0, root_rows * n_dp // 512, root_step, 0)

    def mid_step(d):
        who = lax.rem(me + n_dp - d, n_dp)
        mid_copy(d, who).wait_recv()
        mid_block(who)

    over(n_dp, mid_step)

    for j in range(kv_heads):
        r = acc[j]
        y = (r[:, :128] / r[:, 128:]).astype(BF16)
        for g in range(group):
            h = j * group + g
            attn[:, h * 128 : h * 128 + 128] = y[g * height : (g + 1) * height]

    def product(who):
        rows = pl.ds(pl.multiple_of(who * share, share), share)
        return jnp.dot(attn[rows, :], wo[...], preferred_element_type=F32).astype(BF16)

    def send_part(d):
        parts[d] = product(lax.rem(mh + d, n_head))
        part_copy(d, mh).start()

    over(n_head, send_part)
    total = product(mh).astype(F32)
    for d in range(1, n_head):
        who = lax.rem(mh + d, n_head)
        part_copy(d, who).wait_recv()
        total = total + got[who].astype(F32)
    out[...] = total.astype(BF16)

    def finish_dp(d):
        info_copy(d, me).wait_send()
        for copy in root_copies(d, me):
            copy.wait_send()
        mid_copy(d, me).wait_send()

    def finish_head(d):
        hid_copy(d, mh).wait_send()
        part_copy(d, mh).wait_send()

    over(n_dp, finish_dp)
    over(n_head, finish_head)


def body(
    hidden_in, norm_gain, w_query, key_weight, w_value, query_gain, key_gain, w_out,
    prefix_root_keys, prefix_root_values, mid_keys, mid_values, mid_lengths, leaf_keys,
    leaf_values, leaf_lengths, token_request, request_node,
):
    n_dp, n_head = lax.axis_size("dp"), lax.axis_size("head")
    share, model = hidden_in.shape
    height = share * n_head
    qw, kw = w_query.shape[1], key_weight.shape[1]
    kv_heads, group = kw // 128, qw // kw
    requests = request_node.shape[1]
    root_rows = prefix_root_keys.shape[0]
    half = np.arange(64, dtype=np.float32) * np.float32(2.0 / 128)
    freqs = np.power(np.float32(THETA), -half).astype(np.float32)
    freqs = jnp.asarray(np.concatenate([freqs, freqs])[None])
    vmem = pl.BlockSpec(memory_space=pltpu.VMEM)
    hbm = pl.BlockSpec(memory_space=pl.ANY)
    dma = pltpu.SemaphoreType.DMA
    return pl.pallas_call(
        functools.partial(kernel, n_dp, n_head),
        out_shape=(
            jax.ShapeDtypeStruct((share, model), BF16),
            jax.ShapeDtypeStruct((height, kw), BF16),
            jax.ShapeDtypeStruct((height, kw), BF16),
        ),
        in_specs=[vmem, vmem, hbm, hbm, hbm, vmem, vmem, hbm] + [vmem] * 11,
        out_specs=(vmem, vmem, vmem),
        scratch_shapes=[
            pltpu.VMEM(w_query.shape, BF16),
            pltpu.VMEM(key_weight.shape, BF16),
            pltpu.VMEM(w_value.shape, BF16),
            pltpu.VMEM(w_out.shape, BF16),
            pltpu.VMEM((height, model), BF16),
            pltpu.VMEM((n_dp, requests, 128), F32),
            pltpu.VMEM((n_dp * root_rows, kw), BF16),
            pltpu.VMEM((n_dp * root_rows, kw), BF16),
            pltpu.VMEM((n_dp, MID_LEN, 2 * kw), BF16),
            pltpu.VMEM((n_dp, MID_LEN, 2 * kw), BF16),
            pltpu.VMEM((kv_heads, group * height, 128), BF16),
            pltpu.VMEM((height, 128), BF16),
            pltpu.VMEM((kv_heads, group * height, 128), F32),
            pltpu.VMEM((kv_heads, group * height, 256), F32),
            pltpu.VMEM((height, qw), BF16),
            pltpu.VMEM((n_head, share, model), BF16),
            pltpu.VMEM((n_head, share, model), BF16),
            dma((4,)),
            dma((n_head,)), dma((n_head,)),
            dma((n_dp,)), dma((n_dp,)),
            dma((n_dp,)), dma((n_dp,)),
            dma((n_dp,)), dma((n_dp,)),
            dma((n_dp,)), dma((n_dp,)),
            dma((n_head,)), dma((n_head,)),
        ],
        compiler_params=pltpu.CompilerParams(
            collective_id=0, has_side_effects=True, vmem_limit_bytes=56 * 2**20
        ),
    )(
        hidden_in, norm_gain[None], w_query, key_weight, w_value, query_gain[None],
        key_gain[None], w_out, prefix_root_keys, prefix_root_values, mid_keys, mid_values,
        mid_lengths[None], leaf_keys, leaf_values, leaf_lengths[None], token_request,
        request_node, freqs,
    )


def solution(mesh):
    shard = P("dp", "head")
    tokens = P(("dp", "head"), None)
    in_specs = (
        tokens, P(), P(None, "head"), P(None, "head"), P(None, "head"), P(), P(),
        P("head", None), shard, shard, shard, shard, P(), shard, shard, P("dp"),
        P("dp", None), P("dp", None),
    )
    return jax.shard_map(
        body, mesh=mesh, in_specs=in_specs, out_specs=(tokens, shard, shard), check_vma=False
    )
```

```python
import functools
import math

import jax
import jax.numpy as jnp
import numpy as np
from jax import lax
from jax.experimental import pallas as pl
from jax.experimental.pallas import tpu as pltpu
from jax.sharding import PartitionSpec as P

MID_DEV = 2
MID_LEN = 256
EPS = 1e-06
THETA = 1000000.0
MASKED = -1e30
F32 = jnp.float32
BF16 = jnp.bfloat16
MESH = pl.DeviceIdType.MESH


def kernel(
    n_dp, n_head,
    hidden, norm_gain, wq_hbm, wk_hbm, wv_hbm, query_gain, key_gain, wo_hbm, root_k, root_v,
    mid_k, mid_v, mid_len, leaf_k, leaf_v, leaf_len, seg_in, node_in, freqs,
    out, new_k, new_v,
    wq, wk, wv, wo, normed, info, roots_k, roots_v, staged, mids, queries, tags, top, acc, attn,
    parts, got, local_sem, hid_send, hid_recv, info_send, info_recv, rk_send, rk_recv, rv_send,
    rv_recv, mid_send, mid_recv, part_send, part_recv,
):
    me, mh = lax.axis_index("dp"), lax.axis_index("head")
    share = hidden.shape[0]
    height = normed.shape[0]
    requests = node_in.shape[1]
    nodes = mid_len.shape[1]
    root_rows = root_k.shape[0]
    kv_heads = wk.shape[1] // 128
    group = wq.shape[1] // wk.shape[1]
    kw = wk.shape[1]
    scale = 1.0 / math.sqrt(128)

    loads = [
        pltpu.make_async_copy(a, b, local_sem.at[i])
        for i, (a, b) in enumerate(((wq_hbm, wq), (wk_hbm, wk), (wv_hbm, wv), (wo_hbm, wo)))
    ]
    for load in loads:
        load.start()

    barrier = pltpu.get_barrier_semaphore()

    def greet_dp(d, _):
        pl.semaphore_signal(
            barrier, inc=1, device_id=(lax.rem(me + d, n_dp), mh), device_id_type=MESH
        )
        return 0

    def greet_head(d, _):
        pl.semaphore_signal(
            barrier, inc=1, device_id=(me, lax.rem(mh + d, n_head)), device_id_type=MESH
        )
        return 0

    lax.fori_loop(1, n_dp, greet_dp, 0)
    lax.fori_loop(1, n_head, greet_head, 0)

    x = hidden[...].astype(F32)
    power = jnp.mean(x * x, axis=-1, keepdims=True)
    x = (x * lax.rsqrt(power + EPS) * norm_gain[...].astype(F32)).astype(BF16)
    my_rows = pl.ds(pl.multiple_of(mh * share, share), share)
    normed[my_rows, :] = x

    eye = lax.broadcasted_iota(jnp.int32, (requests, requests), 0) == lax.broadcasted_iota(
        jnp.int32, (requests, requests), 1
    )

    def column(row):
        return jnp.sum(jnp.where(eye, row.astype(F32), 0.0), axis=1, keepdims=True)

    branch = column(node_in[...])
    info[me] = jnp.broadcast_to(branch, (requests, 128))
    my_root = pl.ds(pl.multiple_of(me * root_rows, root_rows), root_rows)
    roots_k[my_root, :] = root_k[...]
    roots_v[my_root, :] = root_v[...]

    pl.semaphore_wait(barrier, n_dp + n_head - 2)

    def hid_copy(d, source):
        rows = pl.ds(pl.multiple_of(source * share, share), share)
        return pltpu.make_async_remote_copy(
            normed.at[rows, :], normed.at[rows, :], hid_send.at[d], hid_recv.at[source],
            device_id=(me, lax.rem(mh + d, n_head)), device_id_type=MESH,
        )

    def info_copy(d, source):
        return pltpu.make_async_remote_copy(
            info.at[source], info.at[source], info_send.at[d], info_recv.at[source],
            device_id=(lax.rem(me + d, n_dp), mh), device_id_type=MESH,
        )

    def flipped(d):
        other = me
        for k in range(n_dp.bit_length() - 1):
            if d >> k & 1:
                other = other + (1 - 2 * lax.rem(me // 2**k, 2)) * 2**k
        return other

    def root_copies(d, block):
        low = d & -d
        rows = pl.ds(pl.multiple_of(block * root_rows, root_rows), root_rows)
        target = (flipped(low), mh)
        return [
            pltpu.make_async_remote_copy(
                held.at[rows, :], held.at[rows, :], send.at[d], recv.at[d],
                device_id=target, device_id_type=MESH,
            )
            for held, send, recv in ((roots_k, rk_send, rk_recv), (roots_v, rv_send, rv_recv))
        ]

    def relay(low):
        for d in range(low, n_dp, 2 * low):
            block = d - low
            if block & -block == 2 * low:
                for copy in root_copies(block, flipped(block)):
                    copy.wait_recv()
            for copy in root_copies(d, flipped(block)):
                copy.start()

    def mid_copy(d, source):
        return pltpu.make_async_remote_copy(
            staged.at[d], mids.at[source], mid_send.at[d], mid_recv.at[source],
            device_id=(lax.rem(me + d, n_dp), mh), device_id_type=MESH,
        )

    def part_copy(d, source):
        return pltpu.make_async_remote_copy(
            parts.at[d], got.at[source], part_send.at[d], part_recv.at[source],
            device_id=(me, lax.rem(mh + d, n_head)), device_id_type=MESH,
        )

    def over(count, act):
        def step(d, _):
            act(d)
            return 0

        lax.fori_loop(1, count, step, 0)

    over(n_dp, lambda d: info_copy(d, me).start())
    over(n_head, lambda d: hid_copy(d, mh).start())

    hops = [n_dp >> k for k in range(1, n_dp.bit_length())]
    relay(hops[0])

    def chosen(who):
        wish = jnp.max(jnp.where(info[who] == (MID_DEV * me + 1).astype(F32), 1.0, 0.0), axis=0, keepdims=True)
        wish = jnp.max(wish, axis=1, keepdims=True)
        pair = [
            jnp.concatenate([mid_k[pl.ds(s * MID_LEN, MID_LEN), :], mid_v[pl.ds(s * MID_LEN, MID_LEN), :]], axis=1).astype(F32)
            for s in range(2)
        ]
        wide = jnp.broadcast_to(wish, pair[0].shape)
        return jnp.where(wide > 0.5, pair[1], pair[0]).astype(BF16)

    def send_mid(d):
        who = lax.rem(me + d, n_dp)
        info_copy(d, who).wait_recv()
        staged[d] = chosen(who)
        mid_copy(d, me).start()

    over(n_dp, send_mid)
    mids[me] = chosen(me)
    relay(hops[1])

    seg = seg_in[...].astype(F32)
    req = lax.broadcasted_iota(jnp.int32, (requests, height), 0).astype(F32)
    starts = jnp.sum(jnp.where(seg < req, 1.0, 0.0), axis=1, keepdims=True)
    node_ids = lax.broadcasted_iota(jnp.int32, (requests, nodes), 1).astype(F32)
    branch_len = jnp.sum(
        jnp.where(node_ids == branch, mid_len[...].astype(F32), 0.0), axis=1, keepdims=True
    )
    leaf_col = column(leaf_len[...])
    base = root_rows * n_dp + branch_len + leaf_col - starts
    pos = jnp.sum(jnp.where(seg == req, base, 0.0), axis=0, keepdims=True)
    pos = pos + lax.broadcasted_iota(jnp.int32, (1, height), 1).astype(F32)
    pos = jnp.transpose(jnp.broadcast_to(pos, (128, height)))
    seg_rep = jnp.transpose(jnp.broadcast_to(seg, (128, height)))
    lane = lax.broadcasted_iota(jnp.int32, (height, 128), 1)
    tags[...] = jnp.where(seg_rep == lane.astype(F32), 1.0, 0.0).astype(BF16)
    spread = lax.broadcasted_iota(jnp.int32, (requests, 128), 0) == lax.broadcasted_iota(
        jnp.int32, (requests, 128), 1
    )

    def lanes(col):
        return jnp.sum(jnp.where(spread, col, 0.0), axis=0, keepdims=True)

    real = jnp.sum(jnp.where(spread, 1.0, 0.0), axis=0, keepdims=True)
    leaf_row, mid_row, node_row = lanes(leaf_col), lanes(branch_len), lanes(branch)
    node_row = jnp.where(real > 0.5, node_row, -2.0)
    angle = pos * freqs[...]
    cosine = jnp.cos(angle)
    sine = jnp.sin(angle)
    sine = jnp.where(lane < 64, -sine, sine)

    over(n_head, lambda d: hid_copy(d, lax.rem(mh + d, n_head)).wait_recv())
    for load in loads:
        load.wait()
    inputs = normed[...]
    values = jnp.dot(inputs, wv[...], preferred_element_type=F32).astype(BF16)
    new_v[...] = values

    def turned(y, gain):
        power = jnp.mean(y * y, axis=-1, keepdims=True)
        y = y * lax.rsqrt(power + EPS) * gain[...].astype(F32)
        return (y * cosine + pltpu.roll(y, 64, axis=1) * sine).astype(BF16)

    for j in range(kv_heads):
        cols = slice(j * 128, j * 128 + 128)
        y = jnp.dot(inputs, wk[:, cols], preferred_element_type=F32)
        new_k[:, cols] = turned(y, key_gain)
    for j in range(kv_heads):
        for g in range(group):
            h = j * group + g
            y = jnp.dot(inputs, wq[:, h * 128 : h * 128 + 128], preferred_element_type=F32)
            queries[j, g * height : (g + 1) * height, :] = turned(y, query_gain)

    for hop in hops[2:]:
        relay(hop)
    tall = group * height

    def attend(j, keys, bias, vals, first=False, causal=False):
        q = queries[j]
        if bias is not None:
            q = jnp.concatenate([q, jnp.concatenate([tags[...]] * group, axis=0)], axis=1)
            keys = jnp.concatenate([keys, bias], axis=1)
        s = lax.dot_general(q, keys, (((1,), (1,)), ((), ())), preferred_element_type=F32)
        if causal:
            row = lax.broadcasted_iota(jnp.int32, (tall, height), 0) % height
            s = jnp.where(lax.broadcasted_iota(jnp.int32, (tall, height), 1) <= row, s, MASKED)
        peak = jnp.max(s, axis=1, keepdims=True)
        if not first:
            old = top[j]
            peak = jnp.maximum(old[:, :1], peak)
        p = jnp.exp((s - peak) * scale).astype(BF16)
        wide = jnp.concatenate([vals, jnp.ones((vals.shape[0], 128), BF16)], axis=1)
        r = jnp.dot(p, wide, preferred_element_type=F32)
        full = jnp.broadcast_to(peak, (tall, 128))
        if not first:
            shrink = jnp.exp((old - full) * scale)
            r = acc[j] * jnp.concatenate([shrink, shrink], axis=1) + r
        acc[j] = r
        top[j] = full

    key_row = lax.broadcasted_iota(jnp.int32, (height, 128), 0)
    own_bias = jnp.where(tags[...].astype(F32) > 0.5, 0.0, MASKED).astype(BF16)
    for j in range(kv_heads):
        cols = slice(j * 128, j * 128 + 128)
        attend(j, new_k[:, cols], own_bias, new_v[:, cols], first=True, causal=True)
    leaf_each = leaf_k.shape[0] // requests

    def leaf_step(i, _):
        rows = pl.ds(pl.multiple_of(i * 256, 256), 256)
        at = lax.broadcasted_iota(jnp.int32, (256, 128), 0) + i * 256
        mine = lax.broadcasted_iota(jnp.int32, (256, 128), 1) == at // leaf_each
        live = (at % leaf_each).astype(F32) < leaf_row
        bias = jnp.where(mine & live, 0.0, MASKED).astype(BF16)
        for j in range(kv_heads):
            cols = slice(j * 128, j * 128 + 128)
            attend(j, leaf_k[rows, cols], bias, leaf_v[rows, cols])
        return 0

    lax.fori_loop(0, leaf_k.shape[0] // 256, leaf_step, 0)

    def mid_block(who):
        at = lax.broadcasted_iota(jnp.int32, (MID_LEN, 128), 0).astype(F32)
        first_node = (MID_DEV * who).astype(F32)
        mine = (node_row >= first_node) & (node_row < first_node + MID_DEV)
        reach = jnp.where(mine, mid_row, 0.0)
        bias = jnp.where(at < reach, 0.0, MASKED).astype(BF16)
        block = mids.at[who]
        for j in range(kv_heads):
            attend(
                j, block[:, j * 128 : j * 128 + 128], bias,
                block[:, kw + j * 128 : kw + j * 128 + 128],
            )

    mid_block(me)

    for d in range(1, n_dp, 2):
        for copy in root_copies(d, flipped(d)):
            copy.wait_recv()

    def root_step(i, _):
        rows = pl.ds(pl.multiple_of(i * 512, 512), 512)
        for j in range(kv_heads):
            cols = slice(j * 128, j * 128 + 128)
            attend(j, roots_k[rows, cols], None, roots_v[rows, cols])
        return 0

    lax.fori_loop(0, root_rows * n_dp // 512, root_step, 0)

    def mid_step(d):
        who = lax.rem(me + n_dp - d, n_dp)
        mid_copy(d, who).wait_recv()
        mid_block(who)

    over(n_dp, mid_step)

    for j in range(kv_heads):
        r = acc[j]
        y = (r[:, :128] / r[:, 128:]).astype(BF16)
        for g in range(group):
            h = j * group + g
            attn[:, h * 128 : h * 128 + 128] = y[g * height : (g + 1) * height]

    def product(who):
        rows = pl.ds(pl.multiple_of(who * share, share), share)
        return jnp.dot(attn[rows, :], wo[...], preferred_element_type=F32).astype(BF16)

    def send_part(d):
        parts[d] = product(lax.rem(mh + d, n_head))
        part_copy(d, mh).start()

    over(n_head, send_part)
    total = product(mh).astype(F32)
    for d in range(1, n_head):
        who = lax.rem(mh + d, n_head)
        part_copy(d, who).wait_recv()
        total = total + got[who].astype(F32)
    out[...] = total.astype(BF16)

    def finish_dp(d):
        info_copy(d, me).wait_send()
        mid_copy(d, me).wait_send()

    def finish_head(d):
        hid_copy(d, mh).wait_send()
        part_copy(d, mh).wait_send()

    over(n_dp, finish_dp)
    for d in range(1, n_dp):
        for copy in root_copies(d, flipped(d - (d & -d))):
            copy.wait_send()
    over(n_head, finish_head)


def body(
    hidden_in, norm_gain, w_query, key_weight, w_value, query_gain, key_gain, w_out,
    prefix_root_keys, prefix_root_values, mid_keys, mid_values, mid_lengths, leaf_keys,
    leaf_values, leaf_lengths, token_request, request_node,
):
    n_dp, n_head = lax.axis_size("dp"), lax.axis_size("head")
    share, model = hidden_in.shape
    height = share * n_head
    qw, kw = w_query.shape[1], key_weight.shape[1]
    kv_heads, group = kw // 128, qw // kw
    requests = request_node.shape[1]
    root_rows = prefix_root_keys.shape[0]
    half = np.arange(64, dtype=np.float32) * np.float32(2.0 / 128)
    freqs = np.power(np.float32(THETA), -half).astype(np.float32)
    freqs = jnp.asarray(np.concatenate([freqs, freqs])[None])
    vmem = pl.BlockSpec(memory_space=pltpu.VMEM)
    hbm = pl.BlockSpec(memory_space=pl.ANY)
    dma = pltpu.SemaphoreType.DMA
    return pl.pallas_call(
        functools.partial(kernel, n_dp, n_head),
        out_shape=(
            jax.ShapeDtypeStruct((share, model), BF16),
            jax.ShapeDtypeStruct((height, kw), BF16),
            jax.ShapeDtypeStruct((height, kw), BF16),
        ),
        in_specs=[vmem, vmem, hbm, hbm, hbm, vmem, vmem, hbm] + [vmem] * 11,
        out_specs=(vmem, vmem, vmem),
        scratch_shapes=[
            pltpu.VMEM(w_query.shape, BF16),
            pltpu.VMEM(key_weight.shape, BF16),
            pltpu.VMEM(w_value.shape, BF16),
            pltpu.VMEM(w_out.shape, BF16),
            pltpu.VMEM((height, model), BF16),
            pltpu.VMEM((n_dp, requests, 128), F32),
            pltpu.VMEM((n_dp * root_rows, kw), BF16),
            pltpu.VMEM((n_dp * root_rows, kw), BF16),
            pltpu.VMEM((n_dp, MID_LEN, 2 * kw), BF16),
            pltpu.VMEM((n_dp, MID_LEN, 2 * kw), BF16),
            pltpu.VMEM((kv_heads, group * height, 128), BF16),
            pltpu.VMEM((height, 128), BF16),
            pltpu.VMEM((kv_heads, group * height, 128), F32),
            pltpu.VMEM((kv_heads, group * height, 256), F32),
            pltpu.VMEM((height, qw), BF16),
            pltpu.VMEM((n_head, share, model), BF16),
            pltpu.VMEM((n_head, share, model), BF16),
            dma((4,)),
            dma((n_head,)), dma((n_head,)),
            dma((n_dp,)), dma((n_dp,)),
            dma((n_dp,)), dma((n_dp,)),
            dma((n_dp,)), dma((n_dp,)),
            dma((n_dp,)), dma((n_dp,)),
            dma((n_head,)), dma((n_head,)),
        ],
        compiler_params=pltpu.CompilerParams(
            collective_id=0, has_side_effects=True, vmem_limit_bytes=56 * 2**20
        ),
    )(
        hidden_in, norm_gain[None], w_query, key_weight, w_value, query_gain[None],
        key_gain[None], w_out, prefix_root_keys, prefix_root_values, mid_keys, mid_values,
        mid_lengths[None], leaf_keys, leaf_values, leaf_lengths[None], token_request,
        request_node, freqs,
    )


def solution(mesh):
    shard = P("dp", "head")
    tokens = P(("dp", "head"), None)
    in_specs = (
        tokens, P(), P(None, "head"), P(None, "head"), P(None, "head"), P(), P(),
        P("head", None), shard, shard, shard, shard, P(), shard, shard, P("dp"),
        P("dp", None), P("dp", None),
    )
    return jax.shard_map(
        body, mesh=mesh, in_specs=in_specs, out_specs=(tokens, shard, shard), check_vma=False
    )
```

```python
import functools
import math

import jax
import jax.numpy as jnp
import numpy as np
from jax import lax
from jax.experimental import pallas as pl
from jax.experimental.pallas import tpu as pltpu
from jax.sharding import PartitionSpec as P

MID_DEV = 2
MID_LEN = 256
EPS = 1e-06
THETA = 1000000.0
MASKED = -1e30
F32 = jnp.float32
BF16 = jnp.bfloat16
MESH = pl.DeviceIdType.MESH


def kernel(
    n_dp, n_head,
    hidden, norm_gain, wq_hbm, wk_hbm, wv_hbm, query_gain, key_gain, wo_hbm, root_k, root_v,
    mid_k, mid_v, mid_len, leaf_k, leaf_v, leaf_len, seg_in, node_in, freqs,
    out, new_k, new_v,
    wq, wk, wv, wo, normed, info, roots_k, roots_v, staged, mids, queries, tags, top, acc, attn,
    parts, got, local_sem, hid_send, hid_recv, info_send, info_recv, rk_send, rk_recv, rv_send,
    rv_recv, mid_send, mid_recv, part_send, part_recv,
):
    me, mh = lax.axis_index("dp"), lax.axis_index("head")
    share = hidden.shape[0]
    height = normed.shape[0]
    requests = node_in.shape[1]
    nodes = mid_len.shape[1]
    root_rows = root_k.shape[0]
    kv_heads = wk.shape[1] // 128
    group = wq.shape[1] // wk.shape[1]
    kw = wk.shape[1]
    scale = 1.0 / math.sqrt(128)

    loads = [
        pltpu.make_async_copy(a, b, local_sem.at[i])
        for i, (a, b) in enumerate(((wq_hbm, wq), (wk_hbm, wk), (wv_hbm, wv), (wo_hbm, wo)))
    ]
    for load in loads:
        load.start()

    barrier = pltpu.get_barrier_semaphore()

    def greet_dp(d, _):
        pl.semaphore_signal(
            barrier, inc=1, device_id=(lax.rem(me + d, n_dp), mh), device_id_type=MESH
        )
        return 0

    def greet_head(d, _):
        pl.semaphore_signal(
            barrier, inc=1, device_id=(me, lax.rem(mh + d, n_head)), device_id_type=MESH
        )
        return 0

    lax.fori_loop(1, n_dp, greet_dp, 0)
    lax.fori_loop(1, n_head, greet_head, 0)

    eye = lax.broadcasted_iota(jnp.int32, (requests, requests), 0) == lax.broadcasted_iota(
        jnp.int32, (requests, requests), 1
    )

    def column(row):
        return jnp.sum(jnp.where(eye, row.astype(F32), 0.0), axis=1, keepdims=True)

    branch = column(node_in[...])
    info[me] = jnp.broadcast_to(branch, (requests, 128))
    my_root = pl.ds(pl.multiple_of(me * root_rows, root_rows), root_rows)
    roots_k[my_root, :] = root_k[...]
    roots_v[my_root, :] = root_v[...]

    pl.semaphore_wait(barrier, n_dp + n_head - 2)

    def hid_copy(d, source):
        rows = pl.ds(pl.multiple_of(source * share, share), share)
        return pltpu.make_async_remote_copy(
            normed.at[rows, :], normed.at[rows, :], hid_send.at[d], hid_recv.at[source],
            device_id=(me, lax.rem(mh + d, n_head)), device_id_type=MESH,
        )

    def info_copy(d, source):
        return pltpu.make_async_remote_copy(
            info.at[source], info.at[source], info_send.at[d], info_recv.at[source],
            device_id=(lax.rem(me + d, n_dp), mh), device_id_type=MESH,
        )

    def flipped(d):
        other = me
        for k in range(n_dp.bit_length() - 1):
            if d >> k & 1:
                other = other + (1 - 2 * lax.rem(me // 2**k, 2)) * 2**k
        return other

    def root_copies(d, block):
        low = d & -d
        rows = pl.ds(pl.multiple_of(block * root_rows, root_rows), root_rows)
        target = (flipped(low), mh)
        return [
            pltpu.make_async_remote_copy(
                held.at[rows, :], held.at[rows, :], send.at[d], recv.at[d],
                device_id=target, device_id_type=MESH,
            )
            for held, send, recv in ((roots_k, rk_send, rk_recv), (roots_v, rv_send, rv_recv))
        ]

    def relay(low):
        for d in range(low, n_dp, 2 * low):
            block = d - low
            if block & -block == 2 * low:
                for copy in root_copies(block, flipped(block)):
                    copy.wait_recv()
            for copy in root_copies(d, flipped(block)):
                copy.start()

    def mid_copy(d, source):
        return pltpu.make_async_remote_copy(
            staged.at[d], mids.at[source], mid_send.at[d], mid_recv.at[source],
            device_id=(lax.rem(me + d, n_dp), mh), device_id_type=MESH,
        )

    def part_copy(d, source):
        return pltpu.make_async_remote_copy(
            parts.at[d], got.at[source], part_send.at[d], part_recv.at[source],
            device_id=(me, lax.rem(mh + d, n_head)), device_id_type=MESH,
        )

    def over(count, act):
        def step(d, _):
            act(d)
            return 0

        lax.fori_loop(1, count, step, 0)

    over(n_dp, lambda d: info_copy(d, me).start())

    hops = [n_dp >> k for k in range(1, n_dp.bit_length())]
    relay(hops[0])

    x = hidden[...].astype(F32)
    power = jnp.mean(x * x, axis=-1, keepdims=True)
    x = (x * lax.rsqrt(power + EPS) * norm_gain[...].astype(F32)).astype(BF16)
    my_rows = pl.ds(pl.multiple_of(mh * share, share), share)
    normed[my_rows, :] = x

    over(n_head, lambda d: hid_copy(d, mh).start())

    def chosen(who):
        wish = jnp.max(jnp.where(info[who] == (MID_DEV * me + 1).astype(F32), 1.0, 0.0), axis=0, keepdims=True)
        wish = jnp.max(wish, axis=1, keepdims=True)
        pair = [
            jnp.concatenate([mid_k[pl.ds(s * MID_LEN, MID_LEN), :], mid_v[pl.ds(s * MID_LEN, MID_LEN), :]], axis=1).astype(F32)
            for s in range(2)
        ]
        wide = jnp.broadcast_to(wish, pair[0].shape)
        return jnp.where(wide > 0.5, pair[1], pair[0]).astype(BF16)

    def send_mid(d):
        who = lax.rem(me + d, n_dp)
        info_copy(d, who).wait_recv()
        staged[d] = chosen(who)
        mid_copy(d, me).start()

    over(n_dp, send_mid)
    mids[me] = chosen(me)
    relay(hops[1])

    seg = seg_in[...].astype(F32)
    req = lax.broadcasted_iota(jnp.int32, (requests, height), 0).astype(F32)
    starts = jnp.sum(jnp.where(seg < req, 1.0, 0.0), axis=1, keepdims=True)
    node_ids = lax.broadcasted_iota(jnp.int32, (requests, nodes), 1).astype(F32)
    branch_len = jnp.sum(
        jnp.where(node_ids == branch, mid_len[...].astype(F32), 0.0), axis=1, keepdims=True
    )
    leaf_col = column(leaf_len[...])
    base = root_rows * n_dp + branch_len + leaf_col - starts
    pos = jnp.sum(jnp.where(seg == req, base, 0.0), axis=0, keepdims=True)
    pos = pos + lax.broadcasted_iota(jnp.int32, (1, height), 1).astype(F32)
    pos = jnp.transpose(jnp.broadcast_to(pos, (128, height)))
    seg_rep = jnp.transpose(jnp.broadcast_to(seg, (128, height)))
    lane = lax.broadcasted_iota(jnp.int32, (height, 128), 1)
    tags[...] = jnp.where(seg_rep == lane.astype(F32), 1.0, 0.0).astype(BF16)
    spread = lax.broadcasted_iota(jnp.int32, (requests, 128), 0) == lax.broadcasted_iota(
        jnp.int32, (requests, 128), 1
    )

    def lanes(col):
        return jnp.sum(jnp.where(spread, col, 0.0), axis=0, keepdims=True)

    real = jnp.sum(jnp.where(spread, 1.0, 0.0), axis=0, keepdims=True)
    leaf_row, mid_row, node_row = lanes(leaf_col), lanes(branch_len), lanes(branch)
    node_row = jnp.where(real > 0.5, node_row, -2.0)
    angle = pos * freqs[...]
    cosine = jnp.cos(angle)
    sine = jnp.sin(angle)
    sine = jnp.where(lane < 64, -sine, sine)

    over(n_head, lambda d: hid_copy(d, lax.rem(mh + d, n_head)).wait_recv())
    for load in loads:
        load.wait()
    inputs = normed[...]
    values = jnp.dot(inputs, wv[...], preferred_element_type=F32).astype(BF16)
    new_v[...] = values

    def turned(y, gain):
        power = jnp.mean(y * y, axis=-1, keepdims=True)
        y = y * lax.rsqrt(power + EPS) * gain[...].astype(F32)
        return (y * cosine + pltpu.roll(y, 64, axis=1) * sine).astype(BF16)

    for j in range(kv_heads):
        cols = slice(j * 128, j * 128 + 128)
        y = jnp.dot(inputs, wk[:, cols], preferred_element_type=F32)
        new_k[:, cols] = turned(y, key_gain)
    for j in range(kv_heads):
        for g in range(group):
            h = j * group + g
            y = jnp.dot(inputs, wq[:, h * 128 : h * 128 + 128], preferred_element_type=F32)
            queries[j, g * height : (g + 1) * height, :] = turned(y, query_gain)

    for hop in hops[2:]:
        relay(hop)
    tall = group * height

    def attend(j, keys, bias, vals, first=False, causal=False):
        q = queries[j]
        if bias is not None:
            q = jnp.concatenate([q, jnp.concatenate([tags[...]] * group, axis=0)], axis=1)
            keys = jnp.concatenate([keys, bias], axis=1)
        s = lax.dot_general(q, keys, (((1,), (1,)), ((), ())), preferred_element_type=F32)
        if causal:
            row = lax.broadcasted_iota(jnp.int32, (tall, height), 0) % height
            s = jnp.where(lax.broadcasted_iota(jnp.int32, (tall, height), 1) <= row, s, MASKED)
        peak = jnp.max(s, axis=1, keepdims=True)
        if not first:
            old = top[j]
            peak = jnp.maximum(old[:, :1], peak)
        p = jnp.exp((s - peak) * scale).astype(BF16)
        wide = jnp.concatenate([vals, jnp.ones((vals.shape[0], 128), BF16)], axis=1)
        r = jnp.dot(p, wide, preferred_element_type=F32)
        full = jnp.broadcast_to(peak, (tall, 128))
        if not first:
            shrink = jnp.exp((old - full) * scale)
            r = acc[j] * jnp.concatenate([shrink, shrink], axis=1) + r
        acc[j] = r
        top[j] = full

    key_row = lax.broadcasted_iota(jnp.int32, (height, 128), 0)
    own_bias = jnp.where(tags[...].astype(F32) > 0.5, 0.0, MASKED).astype(BF16)
    for j in range(kv_heads):
        cols = slice(j * 128, j * 128 + 128)
        attend(j, new_k[:, cols], own_bias, new_v[:, cols], first=True, causal=True)
    leaf_each = leaf_k.shape[0] // requests

    def leaf_step(i, _):
        rows = pl.ds(pl.multiple_of(i * 256, 256), 256)
        at = lax.broadcasted_iota(jnp.int32, (256, 128), 0) + i * 256
        mine = lax.broadcasted_iota(jnp.int32, (256, 128), 1) == at // leaf_each
        live = (at % leaf_each).astype(F32) < leaf_row
        bias = jnp.where(mine & live, 0.0, MASKED).astype(BF16)
        for j in range(kv_heads):
            cols = slice(j * 128, j * 128 + 128)
            attend(j, leaf_k[rows, cols], bias, leaf_v[rows, cols])
        return 0

    lax.fori_loop(0, leaf_k.shape[0] // 256, leaf_step, 0)

    def mid_block(who):
        at = lax.broadcasted_iota(jnp.int32, (MID_LEN, 128), 0).astype(F32)
        first_node = (MID_DEV * who).astype(F32)
        mine = (node_row >= first_node) & (node_row < first_node + MID_DEV)
        reach = jnp.where(mine, mid_row, 0.0)
        bias = jnp.where(at < reach, 0.0, MASKED).astype(BF16)
        block = mids.at[who]
        for j in range(kv_heads):
            attend(
                j, block[:, j * 128 : j * 128 + 128], bias,
                block[:, kw + j * 128 : kw + j * 128 + 128],
            )

    mid_block(me)

    for d in range(1, n_dp, 2):
        for copy in root_copies(d, flipped(d)):
            copy.wait_recv()

    def root_step(i, _):
        rows = pl.ds(pl.multiple_of(i * 512, 512), 512)
        for j in range(kv_heads):
            cols = slice(j * 128, j * 128 + 128)
            attend(j, roots_k[rows, cols], None, roots_v[rows, cols])
        return 0

    lax.fori_loop(0, root_rows * n_dp // 512, root_step, 0)

    def mid_step(d):
        who = lax.rem(me + n_dp - d, n_dp)
        mid_copy(d, who).wait_recv()
        mid_block(who)

    over(n_dp, mid_step)

    for j in range(kv_heads):
        r = acc[j]
        y = (r[:, :128] / r[:, 128:]).astype(BF16)
        for g in range(group):
            h = j * group + g
            attn[:, h * 128 : h * 128 + 128] = y[g * height : (g + 1) * height]

    def product(who):
        rows = pl.ds(pl.multiple_of(who * share, share), share)
        return jnp.dot(attn[rows, :], wo[...], preferred_element_type=F32).astype(BF16)

    def send_part(d):
        parts[d] = product(lax.rem(mh + d, n_head))
        part_copy(d, mh).start()

    over(n_head, send_part)
    total = product(mh).astype(F32)
    for d in range(1, n_head):
        who = lax.rem(mh + d, n_head)
        part_copy(d, who).wait_recv()
        total = total + got[who].astype(F32)
    out[...] = total.astype(BF16)

    def finish_dp(d):
        info_copy(d, me).wait_send()
        mid_copy(d, me).wait_send()

    def finish_head(d):
        hid_copy(d, mh).wait_send()
        part_copy(d, mh).wait_send()

    over(n_dp, finish_dp)
    for d in range(1, n_dp):
        for copy in root_copies(d, flipped(d - (d & -d))):
            copy.wait_send()
    over(n_head, finish_head)


def body(
    hidden_in, norm_gain, w_query, key_weight, w_value, query_gain, key_gain, w_out,
    prefix_root_keys, prefix_root_values, mid_keys, mid_values, mid_lengths, leaf_keys,
    leaf_values, leaf_lengths, token_request, request_node,
):
    n_dp, n_head = lax.axis_size("dp"), lax.axis_size("head")
    share, model = hidden_in.shape
    height = share * n_head
    qw, kw = w_query.shape[1], key_weight.shape[1]
    kv_heads, group = kw // 128, qw // kw
    requests = request_node.shape[1]
    root_rows = prefix_root_keys.shape[0]
    half = np.arange(64, dtype=np.float32) * np.float32(2.0 / 128)
    freqs = np.power(np.float32(THETA), -half).astype(np.float32)
    freqs = jnp.asarray(np.concatenate([freqs, freqs])[None])
    vmem = pl.BlockSpec(memory_space=pltpu.VMEM)
    hbm = pl.BlockSpec(memory_space=pl.ANY)
    dma = pltpu.SemaphoreType.DMA
    return pl.pallas_call(
        functools.partial(kernel, n_dp, n_head),
        out_shape=(
            jax.ShapeDtypeStruct((share, model), BF16),
            jax.ShapeDtypeStruct((height, kw), BF16),
            jax.ShapeDtypeStruct((height, kw), BF16),
        ),
        in_specs=[vmem, vmem, hbm, hbm, hbm, vmem, vmem, hbm] + [vmem] * 11,
        out_specs=(vmem, vmem, vmem),
        scratch_shapes=[
            pltpu.VMEM(w_query.shape, BF16),
            pltpu.VMEM(key_weight.shape, BF16),
            pltpu.VMEM(w_value.shape, BF16),
            pltpu.VMEM(w_out.shape, BF16),
            pltpu.VMEM((height, model), BF16),
            pltpu.VMEM((n_dp, requests, 128), F32),
            pltpu.VMEM((n_dp * root_rows, kw), BF16),
            pltpu.VMEM((n_dp * root_rows, kw), BF16),
            pltpu.VMEM((n_dp, MID_LEN, 2 * kw), BF16),
            pltpu.VMEM((n_dp, MID_LEN, 2 * kw), BF16),
            pltpu.VMEM((kv_heads, group * height, 128), BF16),
            pltpu.VMEM((height, 128), BF16),
            pltpu.VMEM((kv_heads, group * height, 128), F32),
            pltpu.VMEM((kv_heads, group * height, 256), F32),
            pltpu.VMEM((height, qw), BF16),
            pltpu.VMEM((n_head, share, model), BF16),
            pltpu.VMEM((n_head, share, model), BF16),
            dma((4,)),
            dma((n_head,)), dma((n_head,)),
            dma((n_dp,)), dma((n_dp,)),
            dma((n_dp,)), dma((n_dp,)),
            dma((n_dp,)), dma((n_dp,)),
            dma((n_dp,)), dma((n_dp,)),
            dma((n_head,)), dma((n_head,)),
        ],
        compiler_params=pltpu.CompilerParams(
            collective_id=0, has_side_effects=True, vmem_limit_bytes=56 * 2**20
        ),
    )(
        hidden_in, norm_gain[None], w_query, key_weight, w_value, query_gain[None],
        key_gain[None], w_out, prefix_root_keys, prefix_root_values, mid_keys, mid_values,
        mid_lengths[None], leaf_keys, leaf_values, leaf_lengths[None], token_request,
        request_node, freqs,
    )


def solution(mesh):
    shard = P("dp", "head")
    tokens = P(("dp", "head"), None)
    in_specs = (
        tokens, P(), P(None, "head"), P(None, "head"), P(None, "head"), P(), P(),
        P("head", None), shard, shard, shard, shard, P(), shard, shard, P("dp"),
        P("dp", None), P("dp", None),
    )
    return jax.shard_map(
        body, mesh=mesh, in_specs=in_specs, out_specs=(tokens, shard, shard), check_vma=False
    )
```
